768 devices in a mesh: wide: 96 (over z, y), narrow: 8 (over x, core).
Axes of the slice: x: 4, y: 8, z: 12, core: 2. Of those that a mesh axis runs over, the one named last changes fastest.
Arguments:
- crop_hidden: bfloat16 [12288, 2048], P('wide', 'narrow'), may hold values from -6 to 6
- bottleneck_weight: bfloat16 [2048, 384], P('narrow'), may hold values from -0.125 to 0.125
- prototypes: bfloat16 [384, 65536], P(None, 'narrow'), may hold values from -6 to 6
- teacher_scores: bfloat16 [12288, 65536], P('wide', 'narrow'), may hold values from -1 to 1
Outputs:
- grad_hidden: bfloat16 [12288, 2048], P('wide', 'narrow')
- grad_weight: float32 [384, 2048], P('wide', 'narrow')
The draws below stay inside these ranges and needn't reach their ends.
All inputs are finite; a program needn't handle non-finite values.
Results may differ from the reference program's by a relative error of at most 0.0065.
Values may be sent and summed in bfloat16 or wider, within the bound.
A program may use at most 32 MiB of HBM per device.

```python
import jax
import jax.numpy as jnp
from jax import lax

HID = 2048
BOT = 384
PROTO = 65536
ITERS = 3
CROPS = 12288


def block_scale(rng, dims, pieces, low, largest):
    def one(dim, blocks):
        heights = jax.random.uniform(jax.random.fold_in(jax.random.fold_in(rng, 6), dim), (blocks,), jnp.float32, low / len(pieces), largest / len(pieces))
        return jnp.repeat(jnp.exp(heights), dims[dim] // blocks).reshape((-1,) + (1,) * (len(dims) - dim - 1))

    factor_of = one(*pieces[0])
    for cut in pieces[1:]:
        factor_of = factor_of * one(*cut)
    return factor_of


def centred(stream_key, extent, spread, limit, cuts=(), kind=jnp.bfloat16):
    level = block_scale(stream_key, extent, cuts, -0.22, 0.18) if cuts else 1.0
    drawn = jax.random.normal(stream_key, extent, jnp.float32) * spread * level
    return jnp.minimum(jnp.maximum(drawn, -limit), limit).astype(kind)


def setup_inputs(seed: int = 0) -> dict:
    streams_of = jax.random.split(jax.random.key(seed), 5)
    return {
        "crop_hidden": centred(streams_of[0], (CROPS, HID), 1.0, 6.0, ((0, 96), (1, 8))),
        "bottleneck_weight": centred(streams_of[1], (HID, BOT), HID ** -0.5, 0.125, ((0, 8),)),
        "prototypes": centred(streams_of[2], (BOT, PROTO), 1.0, 6.0, ((1, 8),)),
        "teacher_scores": centred(streams_of[3], (CROPS, PROTO), 0.3, 1.0, ((0, 96), (1, 8))),
    }


TEACHER_TEMP = 0.07
STUDENT_TEMP = 0.1

def reference(crop_hidden, bottleneck_weight, prototypes, teacher_scores):
    bottleneck = jnp.dot(crop_hidden, bottleneck_weight, preferred_element_type=jnp.float32)
    inv_norm = lax.rsqrt(lax.optimization_barrier(jnp.sum(bottleneck * bottleneck, 1)) + 1e-06)
    unit_rows = bottleneck * inv_norm[:, None]
    unit_bf16 = unit_rows.astype(jnp.bfloat16)
    width = PROTO // 8
    block_ids = jnp.arange(8, dtype=jnp.int32)

    def columns_of(block_index):
        raw = lax.dynamic_slice_in_dim(prototypes, block_index * width, width, 1).astype(jnp.float32)
        return (raw * lax.rsqrt(lax.optimization_barrier(jnp.sum(raw * raw, 0)) + 1e-06)[None, :]).astype(jnp.bfloat16)

    def teacher_of(block_index):
        raw = lax.dynamic_slice_in_dim(teacher_scores, block_index * width, width, 1).astype(jnp.float32)
        return jnp.exp(raw / TEACHER_TEMP)

    def student_of(block_index):
        return jnp.exp(jnp.dot(unit_bf16, columns_of(block_index), preferred_element_type=jnp.float32) / STUDENT_TEMP)

    def add_total(carry, block_index):
        return (carry + lax.optimization_barrier(jnp.sum(student_of(block_index), 1)), None)
    softmax_total, _ = lax.scan(add_total, jnp.zeros((CROPS,), jnp.float32), block_ids)
    row_scale = jnp.ones((CROPS,), jnp.float32)
    col_scale = jnp.ones((PROTO,), jnp.float32)
    for iteration in range(ITERS):
        column_mass = lax.map(lambda b: lax.optimization_barrier(jnp.sum(teacher_of(b) * row_scale[:, None], 0)), block_ids)
        col_scale = 1.0 / (PROTO * column_mass.reshape(PROTO))

        def add_rows(carry, block_index):
            piece = lax.dynamic_slice_in_dim(col_scale, block_index * width, width, 0)
            return (carry + lax.optimization_barrier(jnp.sum(teacher_of(block_index) * piece[None, :], 1)), None)
        row_mass, _ = lax.scan(add_rows, jnp.zeros((CROPS,), jnp.float32), block_ids)
        row_scale = 1.0 / (CROPS * row_mass)
    scaled_rows = row_scale * CROPS

    def add_grad(carry, block_index):
        piece = lax.dynamic_slice_in_dim(col_scale, block_index * width, width, 0)
        target = teacher_of(block_index) * scaled_rows[:, None] * piece[None, :]
        student_prob = student_of(block_index) / softmax_total[:, None]
        score_grad = (student_prob - target).astype(jnp.bfloat16)
        term = lax.dot_general(score_grad, columns_of(block_index), (((1,), (1,)), ((), ())), preferred_element_type=jnp.float32)
        return (carry + term, None)
    summed, _ = lax.scan(add_grad, jnp.zeros((CROPS, BOT), jnp.float32), block_ids)
    unit_grad = summed / STUDENT_TEMP
    radial = lax.optimization_barrier(jnp.sum(unit_rows * unit_grad, 1))
    bottle_grad = (inv_norm[:, None] * (unit_grad - unit_rows * radial[:, None])).astype(jnp.bfloat16)
    grad_hidden = lax.dot_general(bottle_grad, bottleneck_weight, (((1,), (1,)), ((), ())), preferred_element_type=jnp.float32).astype(jnp.bfloat16)
    grad_weight = lax.dot_general(bottle_grad, crop_hidden, (((0,), (0,)), ((), ())), preferred_element_type=jnp.float32)
    return (grad_hidden, grad_weight)
```

```python
import jax
import jax.numpy as jnp
from jax import lax
from jax.experimental import pallas as pl
from jax.experimental.pallas import tpu as pltpu
from jax.sharding import PartitionSpec as P

PROTO = 65536
CROPS = 12288
BOT = 384
ITERS = 3
TEACHER_TEMP = 0.07
STUDENT_TEMP = 0.1

Z, Y, N = 12, 8, 8
ROWS = CROPS // (Z * Y)
OWN = ROWS // N
COLS = PROTO // N
LANES = 128
PIECE = COLS // Y
SUB = PIECE // LANES
HIDB = 2048 // N
WIDE = BOT + LANES
GROUP = BOT // Y

F32 = jnp.float32
BF16 = jnp.bfloat16
MESH = pl.DeviceIdType.MESH

FAR8 = (4, 3, 5, 2, 6, 1, 7)
NEAR8 = (1, 7, 2, 6, 3, 5, 4)
FAR12 = (6, 5, 7, 4, 8, 3, 9, 2, 10, 1, 11)
NT = (((1,), (1,)), ((), ()))


def kernel(
    x_hbm, w_hbm, p_hbm, t_hbm, gh_ref, gw_ref,
    tin, raw, wv, xall, texp, inv_col, cbuf, yrecv, zsrc, zrecv, vall,
    nsrc, nrecv, ub, bpart, brecv, ball, unit_own, inv_own, sbuf, gbuf,
    egm, egr, eg_own, tgm, tgr, bgall, perm, bts, btr, gwf, gwz, gwr,
    load_sem, proto_sem, send_sem, recv_sem, v_sem, bt_sem,
):
    w = lax.axis_index("wide")
    n = lax.axis_index("narrow")
    z = lax.div(w, Y)
    y = lax.rem(w, Y)

    def dev_y(d):
        return (z * Y + lax.rem(y + d, Y), n)

    def dev_z(d):
        return (lax.rem(z + d, Z) * Y + y, n)

    def dev_n(d):
        return (w, lax.rem(n + d, N))

    barrier = pltpu.get_barrier_semaphore()
    for d in FAR12:
        pl.semaphore_signal(barrier, inc=1, device_id=dev_z(d), device_id_type=MESH)
    for d in FAR8:
        pl.semaphore_signal(barrier, inc=1, device_id=dev_y(d), device_id_type=MESH)
    for d in FAR8:
        pl.semaphore_signal(barrier, inc=1, device_id=dev_n(d), device_id_type=MESH)

    order = [lax.rem(y + d, Y) for d in FAR8] + [y]
    load_x = pltpu.make_async_copy(x_hbm, xall.at[y], load_sem.at[0])
    load_w = pltpu.make_async_copy(w_hbm, wv, load_sem.at[1])
    load_x.start()
    load_w.start()

    def columns(p):
        return pl.ds(pl.multiple_of(p * PIECE, PIECE), PIECE)

    load_t = []
    for k, p in enumerate(order):
        load_t.append(
            pltpu.make_async_copy(t_hbm.at[:, columns(p)], tin.at[p], load_sem.at[2 + k])
        )
        load_t[-1].start()
    load_p = []
    for p in range(Y):
        load_p.append(
            pltpu.make_async_copy(p_hbm.at[:, columns(p)], raw.at[p], proto_sem.at[p])
        )
        load_p[-1].start()

    sends = []

    def send(src, dst, phase, sem, device):
        pltpu.make_async_remote_copy(
            src, dst, send_sem.at[phase], sem, device_id=device, device_id_type=MESH
        ).start()

    def wait_all(ref, sem):
        pltpu.make_async_copy(ref, ref, sem).wait()

    PH_B, PH_U, PH_X, PH_EG, PH_TG, PH_BG, PH_BT, PH_GW, PH_IT = range(9)

    load_x.wait()
    load_w.wait()
    bpart[...] = jnp.dot(xall[y], wv[...], preferred_element_type=F32).reshape(N, OWN, BOT)

    def first_piece(k, p):
        load_t[k].wait()
        for s in range(SUB):
            e = jnp.exp(tin[p, :, s * LANES : (s + 1) * LANES].astype(F32) * (1.0 / TEACHER_TEMP))
            texp[p * SUB + s] = e
            cbuf[0, p, s : s + 1, :] = jnp.sum(e, 0, keepdims=True)

    def mass_piece(it, p, rows):
        for s in range(SUB):
            cbuf[it, p, s : s + 1, :] = jnp.sum(texp[p * SUB + s] * rows, 0, keepdims=True)

    def send_columns(it, k):
        d = FAR8[k]
        send(
            cbuf.at[it, order[k]], yrecv.at[it, d - 1],
            PH_IT + 4 * it, recv_sem.at[PH_IT + 4 * it], dev_y(d),
        )

    def norm_piece(p):
        load_p[p].wait()
        for s in range(SUB):
            c = raw[p, :, s * LANES : (s + 1) * LANES].astype(F32)
            inv_col[p, s : s + 1, :] = lax.rsqrt(jnp.sum(c * c, 0, keepdims=True) + 1e-06)

    def own_rows():
        wait_all(brecv, recv_sem.at[PH_B])
        b = bpart[n]
        for d in range(N - 1):
            b = b + brecv[d]
        inv = lax.rsqrt(jnp.sum(b * b, 1, keepdims=True) + 1e-06)
        unit = b * inv
        unit_own[...] = unit
        inv_own[...] = jnp.broadcast_to(inv, (OWN, LANES))
        ball[n] = unit.astype(BF16)
        for d in FAR8:
            send(ball.at[n], ball.at[n], PH_U, recv_sem.at[PH_U], dev_n(d))

    def all_rows():
        wait_all(ball.at[pl.ds(0, N - 1)], recv_sem.at[PH_U])

    def student_piece(p):
        sbuf[...] = jnp.dot(
            ball[...].reshape(ROWS, BOT), raw[p], preferred_element_type=F32
        )
        total = jnp.zeros((ROWS, LANES), F32)
        for s in range(SUB):
            at = slice(s * LANES, (s + 1) * LANES)
            inv = inv_col[p, s : s + 1, :]
            e = jnp.exp(sbuf[:, at] * (inv * (1.0 / STUDENT_TEMP)))
            total = total + e
            gbuf[:, at] = (e * inv).astype(BF16)
        part = lax.dot_general(gbuf[...], raw[p], NT, preferred_element_type=F32)
        part = part.reshape(N, OWN, BOT)
        total = total.reshape(N, OWN, LANES)
        if p == 0:
            egm[:, :, :BOT] = part
            egm[:, :, BOT:] = total
        else:
            egm[:, :, :BOT] += part
            egm[:, :, BOT:] += total

    def send_student():
        for d in FAR8:
            send(egm.at[lax.rem(n + d, N)], egr.at[d - 1], PH_EG, recv_sem.at[PH_EG], dev_n(d))

    def own_student():
        wait_all(egr, recv_sem.at[PH_EG])
        e = egm[n]
        for d in range(N - 1):
            e = e + egr[d]
        total = jnp.sum(e[:, BOT:], 1, keepdims=True)
        eg_own[...] = e[:, :BOT] / total

    def permutation():
        k = lax.broadcasted_iota(jnp.int32, (BOT, BOT), 0)
        c = lax.broadcasted_iota(jnp.int32, (BOT, BOT), 1)
        per = GROUP // Z
        ky = lax.div(k, GROUP)
        kz = lax.div(lax.rem(k, GROUP), per)
        kb = lax.rem(k, per)
        perm[...] = jnp.where(c == kz * (per * Y) + ky * per + kb, 1.0, 0.0).astype(BF16)

    def share_hidden(*ds):
        for d in ds:
            send(xall.at[y], xall.at[y], PH_X, recv_sem.at[PH_X], dev_y(d))

    work = {
        (0, "y"): [lambda p=p: norm_piece(p) for p in range(Y)],
        (0, "z"): [lambda: share_hidden(1, 7, 2, 6), own_rows],
        (0, "v"): [all_rows, lambda: student_piece(0), lambda: student_piece(1)],
        (0, "n"): [lambda: student_piece(2), lambda: student_piece(3)],
        (1, "y"): [lambda: student_piece(4), lambda: student_piece(5)],
        (1, "z"): [
            lambda: share_hidden(3, 5),
            lambda: student_piece(6), lambda: student_piece(7), send_student,
        ],
        (1, "v"): [],
        (1, "n"): [permutation],
        (2, "y"): [own_student],
        (2, "z"): [lambda: share_hidden(4)],
        (2, "v"): [],
    }

    def beside(it, name):
        for item in work[(it, name)]:
            item()

    for it in range(ITERS):
        ph = PH_IT + 4 * it
        if it == 0:
            for k in range(Y):
                first_piece(k, order[k])
            pl.semaphore_wait(barrier, (Z - 1) + (Y - 1) + (N - 1))
            for k in range(Y - 1):
                send_columns(0, k)
            for d in FAR8:
                send(bpart.at[lax.rem(n + d, N)], brecv.at[d - 1], PH_B, recv_sem.at[PH_B], dev_n(d))
        else:
            rows = ub[...]
            for k in range(Y):
                mass_piece(it, order[k], rows)
                if k < Y - 1:
                    send_columns(it, k)
        beside(it, "y")
        wait_all(yrecv.at[it], recv_sem.at[ph])
        mass = cbuf[it, y]
        for d in range(Y - 1):
            mass = mass + yrecv[it, d]
        zsrc[it] = mass
        for d in FAR12:
            send(zsrc.at[it], zrecv.at[it, d - 1], ph + 1, recv_sem.at[ph + 1], dev_z(d))
        beside(it, "z")
        wait_all(zrecv.at[it], recv_sem.at[ph + 1])
        for d in range(Z - 1):
            mass = mass + zrecv[it, d]
        vall[it, y] = 1.0 / (PROTO * mass)
        for d in FAR8:
            send(vall.at[it, y], vall.at[it, y], ph + 2, v_sem.at[it, d - 1], dev_y(d))
        beside(it, "v")

        acc = jnp.zeros((ROWS, LANES), F32)
        for k, d in enumerate((0,) + NEAR8):
            p = lax.rem(y - d + Y, Y)
            if d:
                wait_all(vall.at[it, p], v_sem.at[it, d - 1])
            if it < ITERS - 1:
                for s in range(SUB):
                    acc = acc + texp[p * SUB + s] * vall[it, p, s : s + 1, :]
            else:
                for s in range(SUB):
                    tv = texp[p * SUB + s] * vall[it, p, s : s + 1, :]
                    acc = acc + tv
                    gbuf[:, s * LANES : (s + 1) * LANES] = (tv * inv_col[p, s : s + 1, :]).astype(BF16)
                part = lax.dot_general(gbuf[...], raw[p], NT, preferred_element_type=F32)
                part = part.reshape(N, OWN, BOT)
                if k == 0:
                    tgm[:, :, :BOT] = part
                else:
                    tgm[:, :, :BOT] += part
        if it < ITERS - 1:
            nsrc[it] = jnp.sum(acc.T, 0, keepdims=True)
            for d in FAR8:
                send(nsrc.at[it], nrecv.at[it, d - 1], ph + 3, recv_sem.at[ph + 3], dev_n(d))
            beside(it, "n")
            wait_all(nrecv.at[it], recv_sem.at[ph + 3])
            total = nsrc[it]
            for d in range(N - 1):
                total = total + nrecv[it, d]
            scale = 1.0 / (CROPS * total)
            ub[...] = jnp.broadcast_to(scale, (LANES, ROWS)).T
        else:
            tgm[:, :, BOT:] = acc.reshape(N, OWN, LANES)

    for d in FAR8:
        send(tgm.at[lax.rem(n + d, N)], tgr.at[d - 1], PH_TG, recv_sem.at[PH_TG], dev_n(d))
    wait_all(tgr, recv_sem.at[PH_TG])
    t = tgm[n]
    for d in range(N - 1):
        t = t + tgr[d]
    scale = 1.0 / (CROPS * jnp.sum(t[:, BOT:], 1, keepdims=True))
    unit = unit_own[...]
    ug = (eg_own[...] - t[:, :BOT] * (scale * CROPS)) * (1.0 / STUDENT_TEMP)
    radial = jnp.sum(unit * ug, 1, keepdims=True)
    bgall[n] = (inv_own[:, :1] * (ug - unit * radial)).astype(BF16)
    for d in FAR8:
        send(bgall.at[n], bgall.at[n], PH_BG, recv_sem.at[PH_BG], dev_n(d))
    wait_all(bgall.at[pl.ds(0, N - 1)], recv_sem.at[PH_BG])

    bg = bgall[...].reshape(ROWS, BOT)
    bts[...] = (
        lax.dot_general(perm[...], bg, NT, preferred_element_type=F32)
        .astype(BF16)
        .reshape(Y, GROUP, ROWS)
    )
    for d in FAR8:
        send(bts.at[lax.rem(y + d, Y)], btr.at[d - 1], PH_BT, bt_sem.at[d - 1], dev_y(d))
    gh_ref[...] = lax.dot_general(bg, wv[...], NT, preferred_element_type=F32).astype(BF16)
    wait_all(xall.at[pl.ds(0, Y - 1)], recv_sem.at[PH_X])
    gw = jnp.dot(bts[y], xall[y], preferred_element_type=F32)
    for d in NEAR8:
        wait_all(btr.at[d - 1], bt_sem.at[d - 1])
        gw = gw + jnp.dot(btr[d - 1], xall[lax.rem(y - d + Y, Y)], preferred_element_type=F32)
    gwf[...] = gw
    for i in range(Z):
        gwz[i, 0:4, :] = gwf[4 * i : 4 * i + 4, :LANES]
        gwz[i, 4:8, :] = gwf[4 * i : 4 * i + 4, LANES:]
    for d in FAR12:
        send(gwz.at[lax.rem(z + d, Z)], gwr.at[d - 1], PH_GW, recv_sem.at[PH_GW], dev_z(d))
    wait_all(brecv, send_sem.at[PH_B])
    wait_all(ball.at[pl.ds(0, N - 1)], send_sem.at[PH_U])
    wait_all(xall.at[pl.ds(0, Y - 1)], send_sem.at[PH_X])
    wait_all(egr, send_sem.at[PH_EG])
    wait_all(tgr, send_sem.at[PH_TG])
    wait_all(bgall.at[pl.ds(0, N - 1)], send_sem.at[PH_BG])
    wait_all(btr, send_sem.at[PH_BT])
    for it in range(ITERS):
        ph = PH_IT + 4 * it
        wait_all(yrecv.at[it], send_sem.at[ph])
        wait_all(zrecv.at[it], send_sem.at[ph + 1])
        wait_all(vall.at[it, pl.ds(0, Y - 1)], send_sem.at[ph + 2])
        if it < ITERS - 1:
            wait_all(nrecv.at[it], send_sem.at[ph + 3])
    wait_all(gwr, send_sem.at[PH_GW])
    wait_all(gwr, recv_sem.at[PH_GW])
    out = gwz[z]
    for d in range(Z - 1):
        out = out + gwr[d]
    gw_ref[...] = out


def shards(crop_hidden, bottleneck_weight, prototypes, teacher_scores):
    phases = 8 + 4 * ITERS
    vmem = pltpu.VMEM
    gh, gw = pl.pallas_call(
        kernel,
        out_shape=(
            jax.ShapeDtypeStruct((ROWS, HIDB), BF16),
            jax.ShapeDtypeStruct((8, LANES), F32),
        ),
        in_specs=[pl.BlockSpec(memory_space=pl.ANY)] * 4,
        out_specs=(pl.BlockSpec(memory_space=vmem), pl.BlockSpec(memory_space=vmem)),
        scratch_shapes=[
            vmem((Y, ROWS, PIECE), BF16),
            vmem((Y, BOT, PIECE), BF16),
            vmem((HIDB, BOT), BF16),
            vmem((Y, ROWS, HIDB), BF16),
            vmem((Y * SUB, ROWS, LANES), F32),
            vmem((Y, SUB, LANES), F32),
            vmem((ITERS, Y, SUB, LANES), F32),
            vmem((ITERS, Y - 1, SUB, LANES), F32),
            vmem((ITERS, SUB, LANES), F32),
            vmem((ITERS, Z - 1, SUB, LANES), F32),
            vmem((ITERS, Y, SUB, LANES), F32),
            vmem((ITERS - 1, 1, ROWS), F32),
            vmem((ITERS - 1, N - 1, 1, ROWS), F32),
            vmem((ROWS, LANES), F32),
            vmem((N, OWN, BOT), F32),
            vmem((N - 1, OWN, BOT), F32),
            vmem((N, OWN, BOT), BF16),
            vmem((OWN, BOT), F32),
            vmem((OWN, LANES), F32),
            vmem((ROWS, PIECE), F32),
            vmem((ROWS, PIECE), BF16),
            vmem((N, OWN, WIDE), F32),
            vmem((N - 1, OWN, WIDE), F32),
            vmem((OWN, BOT), F32),
            vmem((N, OWN, WIDE), F32),
            vmem((N - 1, OWN, WIDE), F32),
            vmem((N, OWN, BOT), BF16),
            vmem((BOT, BOT), BF16),
            vmem((Y, GROUP, ROWS), BF16),
            vmem((Y - 1, GROUP, ROWS), BF16),
            vmem((GROUP, HIDB), F32),
            vmem((Z, 8, LANES), F32),
            vmem((Z - 1, 8, LANES), F32),
            pltpu.SemaphoreType.DMA((2 + Y,)),
            pltpu.SemaphoreType.DMA((Y,)),
            pltpu.SemaphoreType.DMA((phases,)),
            pltpu.SemaphoreType.DMA((phases,)),
            pltpu.SemaphoreType.DMA((ITERS, Y - 1)),
            pltpu.SemaphoreType.DMA((Y - 1,)),
        ],
        compiler_params=pltpu.CompilerParams(
            collective_id=0, has_side_effects=True, vmem_limit_bytes=60 * 1024 * 1024
        ),
        name="sinkhorn_head",
    )(crop_hidden, bottleneck_weight, prototypes, teacher_scores)
    half = HIDB // 2
    return gh, jnp.concatenate([gw[:4, :half], gw[4:, :half]], axis=1)


def solution(mesh):
    placed = (P("wide", "narrow"), P("narrow", None), P(None, "narrow"), P("wide", "narrow"))
    return jax.shard_map(
        shards,
        mesh=mesh,
        in_specs=placed,
        out_specs=(P("wide", "narrow"), P("wide", "narrow")),
        check_vma=False,
    )
```

```python
import jax
import jax.numpy as jnp
from jax import lax
from jax.experimental import pallas as pl
from jax.experimental.pallas import tpu as pltpu
from jax.sharding import PartitionSpec as P

PROTO = 65536
CROPS = 12288
BOT = 384
ITERS = 3
TEACHER_TEMP = 0.07
STUDENT_TEMP = 0.1

Z, Y, N = 12, 8, 8
ROWS = CROPS // (Z * Y)
OWN = ROWS // N
COLS = PROTO // N
LANES = 128
PIECE = COLS // Y
SUB = PIECE // LANES
HIDB = 2048 // N
WIDE = BOT + LANES
GROUPS = ROWS // 8
TOTALS = 1
GROUP = BOT // Y

F32 = jnp.float32
BF16 = jnp.bfloat16
MESH = pl.DeviceIdType.MESH

FAR8 = (4, 3, 5, 2, 6, 1, 7)
NEAR8 = (1, 7, 2, 6, 3, 5, 4)
FAR12 = (6, 5, 7, 4, 8, 3, 9, 2, 10, 1, 11)
NT = (((1,), (1,)), ((), ()))


def kernel(
    x_hbm, w_hbm, p_hbm, t_hbm, gh_ref, gw_ref,
    tin, raw, wv, xall, texp, inv_col, cbuf, yrecv, zsrc, zrecv, vall,
    nsrc, nrecv, ub, kappa, bpart, brecv, ball, unit_own, inv_own, sbuf, gbuf,
    egm, egr, eg_own, eg_less, tgf, tgm, tgr, bgall, perm, bts, btr, gwf, gwz, gwr,
    load_sem, proto_sem, send_sem, recv_sem, v_sem, bt_sem,
):
    w = lax.axis_index("wide")
    n = lax.axis_index("narrow")
    z = lax.div(w, Y)
    y = lax.rem(w, Y)

    def dev_y(d):
        return (z * Y + lax.rem(y + d, Y), n)

    def dev_z(d):
        return (lax.rem(z + d, Z) * Y + y, n)

    def dev_n(d):
        return (w, lax.rem(n + d, N))

    barrier = pltpu.get_barrier_semaphore()
    for d in FAR12:
        pl.semaphore_signal(barrier, inc=1, device_id=dev_z(d), device_id_type=MESH)
    for d in FAR8:
        pl.semaphore_signal(barrier, inc=1, device_id=dev_y(d), device_id_type=MESH)
    for d in FAR8:
        pl.semaphore_signal(barrier, inc=1, device_id=dev_n(d), device_id_type=MESH)

    order = [lax.rem(y + d, Y) for d in FAR8] + [y]
    load_x = pltpu.make_async_copy(x_hbm, xall.at[y], load_sem.at[0])
    load_w = pltpu.make_async_copy(w_hbm, wv, load_sem.at[1])

    def columns(p):
        return pl.ds(pl.multiple_of(p * PIECE, PIECE), PIECE)

    load_t = []
    for k, p in enumerate(order):
        load_t.append(
            pltpu.make_async_copy(t_hbm.at[:, columns(p)], tin.at[p], load_sem.at[2 + k])
        )
        load_t[-1].start()
    load_x.start()
    load_w.start()
    load_p = []
    for p in range(Y):
        load_p.append(
            pltpu.make_async_copy(p_hbm.at[:, columns(p)], raw.at[p], proto_sem.at[p])
        )
        load_p[-1].start()

    sends = []

    def send(src, dst, phase, sem, device):
        pltpu.make_async_remote_copy(
            src, dst, send_sem.at[phase], sem, device_id=device, device_id_type=MESH
        ).start()

    def wait_all(ref, sem):
        pltpu.make_async_copy(ref, ref, sem).wait()

    PH_B, PH_U, PH_X, PH_EG, PH_TG, PH_BG, PH_BT, PH_GW, PH_IT = range(9)

    def first_piece(k, p):
        load_t[k].wait()
        for s in range(SUB):
            e = jnp.exp(tin[p, :, s * LANES : (s + 1) * LANES].astype(F32) * (1.0 / TEACHER_TEMP))
            texp[p * SUB + s] = e
            cbuf[0, p, s : s + 1, :] = jnp.sum(e, 0, keepdims=True)

    def mass_piece(it, p, rows):
        for s in range(SUB):
            cbuf[it, p, s : s + 1, :] = jnp.sum(texp[p * SUB + s] * rows, 0, keepdims=True)

    def send_columns(it, k):
        d = FAR8[k]
        send(
            cbuf.at[it, order[k]], yrecv.at[it, d - 1],
            PH_IT + 4 * it, recv_sem.at[PH_IT + 4 * it], dev_y(d),
        )

    def norm_piece(p):
        load_p[p].wait()
        for s in range(SUB):
            c = raw[p, :, s * LANES : (s + 1) * LANES].astype(F32)
            inv_col[p, s : s + 1, :] = lax.rsqrt(jnp.sum(c * c, 0, keepdims=True) + 1e-06)

    def own_rows():
        wait_all(brecv, recv_sem.at[PH_B])
        b = bpart[n]
        for d in range(N - 1):
            b = b + brecv[d]
        inv = lax.rsqrt(jnp.sum(b * b, 1, keepdims=True) + 1e-06)
        unit = b * inv
        unit_own[...] = unit
        inv_own[...] = jnp.broadcast_to(inv, (OWN, LANES))
        ball[n] = unit.astype(BF16)
        for d in FAR8:
            send(ball.at[n], ball.at[n], PH_U, recv_sem.at[PH_U], dev_n(d))

    def all_rows():
        wait_all(ball.at[pl.ds(0, N - 1)], recv_sem.at[PH_U])

    def student_piece(p):
        sbuf[...] = jnp.dot(
            ball[...].reshape(ROWS, BOT), raw[p], preferred_element_type=F32
        )
        total = jnp.zeros((ROWS, LANES), F32)
        for s in range(SUB):
            at = slice(s * LANES, (s + 1) * LANES)
            inv = inv_col[p, s : s + 1, :]
            e = jnp.exp(sbuf[:, at] * (inv * (1.0 / STUDENT_TEMP)))
            total = total + e
            gbuf[:, at] = (e * inv).astype(BF16)
        part = lax.dot_general(gbuf[...], raw[p], NT, preferred_element_type=F32)
        part = part.reshape(N, OWN, BOT)
        total = total.reshape(N, OWN, LANES)
        if p == 0:
            egm[:, :, :BOT] = part
            egm[:, :, BOT:] = total
        else:
            egm[:, :, :BOT] += part
            egm[:, :, BOT:] += total

    def send_student():
        for d in FAR8:
            send(egm.at[lax.rem(n + d, N)], egr.at[d - 1], PH_EG, recv_sem.at[PH_EG], dev_n(d))

    def own_student():
        wait_all(egr, recv_sem.at[PH_EG])
        e = egm[n]
        for d in range(N - 1):
            e = e + egr[d]
        total = jnp.sum(e[:, BOT:], 1, keepdims=True)
        eg_own[...] = e[:, :BOT] / total
        eg_less[...] = e[:, :BOT] * kappa[pl.ds(pl.multiple_of(n * OWN, OWN), OWN), :1]

    def permutation():
        k = lax.broadcasted_iota(jnp.int32, (BOT, BOT), 0)
        c = lax.broadcasted_iota(jnp.int32, (BOT, BOT), 1)
        per = GROUP // Z
        ky = lax.div(k, GROUP)
        kz = lax.div(lax.rem(k, GROUP), per)
        kb = lax.rem(k, per)
        perm[...] = jnp.where(c == kz * (per * Y) + ky * per + kb, 1.0, 0.0).astype(BF16)

    def row_tile(a, first):
        lane = lax.broadcasted_iota(jnp.int32, (8, LANES), 1)
        tile = jnp.zeros((8, LANES), F32)
        for g in range(GROUPS):
            mass = jnp.sum(a[8 * g : 8 * g + 8], 1, keepdims=True)
            tile = jnp.where(lane == first + g, mass, tile)
        return tile

    def share_hidden(*ds):
        for d in ds:
            send(xall.at[y], xall.at[y], PH_X, recv_sem.at[PH_X], dev_y(d))

    work = {
        (0, "y"): [lambda p=p: norm_piece(p) for p in range(Y)],
        (0, "z"): [lambda: share_hidden(1, 7, 2, 6), own_rows],
        (0, "v"): [all_rows, lambda: student_piece(0), lambda: student_piece(1)],
        (0, "n"): [lambda: student_piece(2), lambda: student_piece(3)],
        (1, "y"): [lambda: student_piece(4), lambda: student_piece(5)],
        (1, "z"): [
            lambda: share_hidden(3, 5),
            lambda: student_piece(6), lambda: student_piece(7), send_student,
        ],
        (1, "v"): [],
        (1, "n"): [permutation],
        (2, "y"): [own_student],
        (2, "z"): [lambda: share_hidden(4)],
        (2, "v"): [],
    }

    def beside(it, name):
        for item in work[(it, name)]:
            item()

    for it in range(ITERS):
        ph = PH_IT + 4 * it
        if it == 0:
            for k in range(4):
                first_piece(k, order[k])
            pl.semaphore_wait(barrier, (Z - 1) + (Y - 1) + (N - 1))
            for k in range(4):
                send_columns(0, k)
            for k in range(4, Y):
                first_piece(k, order[k])
                if k < Y - 1:
                    send_columns(0, k)
            load_x.wait()
            load_w.wait()
            part = jnp.dot(xall[y], wv[...], preferred_element_type=F32)
            bpart[...] = part.reshape(N, OWN, BOT)
            for d in FAR8:
                send(bpart.at[lax.rem(n + d, N)], brecv.at[d - 1], PH_B, recv_sem.at[PH_B], dev_n(d))
        else:
            rows = ub[...]
            for k in range(Y):
                mass_piece(it, order[k], rows)
                if k < Y - 1:
                    send_columns(it, k)
        beside(it, "y")
        wait_all(yrecv.at[it], recv_sem.at[ph])
        mass = cbuf[it, y]
        for d in range(Y - 1):
            mass = mass + yrecv[it, d]
        zsrc[it] = mass
        for d in FAR12:
            send(zsrc.at[it], zrecv.at[it, d - 1], ph + 1, recv_sem.at[ph + 1], dev_z(d))
        beside(it, "z")
        wait_all(zrecv.at[it], recv_sem.at[ph + 1])
        for d in range(Z - 1):
            mass = mass + zrecv[it, d]
        vall[it, y] = 1.0 / (PROTO * mass)
        for d in FAR8:
            send(vall.at[it, y], vall.at[it, y], ph + 2, v_sem.at[it, d - 1], dev_y(d))
        beside(it, "v")

        acc = jnp.zeros((ROWS, LANES), F32)
        for k, d in enumerate((0,) + NEAR8):
            p = lax.rem(y - d + Y, Y)
            if d:
                wait_all(vall.at[it, p], v_sem.at[it, d - 1])
            if it < ITERS - 1:
                for s in range(SUB):
                    acc = acc + texp[p * SUB + s] * vall[it, p, s : s + 1, :]
            else:
                for s in range(SUB):
                    tv = texp[p * SUB + s] * vall[it, p, s : s + 1, :]
                    acc = acc + tv
                    gbuf[:, s * LANES : (s + 1) * LANES] = (tv * inv_col[p, s : s + 1, :]).astype(BF16)
                part = lax.dot_general(gbuf[...], raw[p], NT, preferred_element_type=F32)
                if k == 0:
                    tgf[...] = part
                else:
                    tgf[...] += part
        if it < ITERS - 1:
            tile = row_tile(acc, 0)
            if it == TOTALS:
                tile = tile + row_tile(egm[:, :, BOT:].reshape(ROWS, LANES), GROUPS)
            nsrc[it] = tile
            for d in FAR8:
                send(nsrc.at[it], nrecv.at[it, d - 1], ph + 3, recv_sem.at[ph + 3], dev_n(d))
            beside(it, "n")
            wait_all(nrecv.at[it], recv_sem.at[ph + 3])
            total = nsrc[it]
            for d in range(N - 1):
                total = total + nrecv[it, d]
            scale = 1.0 / (CROPS * total)
            for g in range(GROUPS):
                ub[8 * g : 8 * g + 8, :] = jnp.broadcast_to(scale[:, g : g + 1], (8, LANES))
            if it == TOTALS:
                for g in range(GROUPS):
                    ratio = scale[:, GROUPS + g : GROUPS + g + 1] / scale[:, g : g + 1]
                    kappa[8 * g : 8 * g + 8, :] = jnp.broadcast_to(ratio, (8, LANES))
        else:
            kap = kappa[...]
            for j in range(BOT // LANES):
                at = slice(j * LANES, (j + 1) * LANES)
                less = tgf[:, at] - kap * egm[:, :, at].reshape(ROWS, LANES)
                tgm[:, :, at] = less.astype(BF16).reshape(N, OWN, LANES)
            high = acc.astype(BF16)
            tgm[:, :, BOT : BOT + LANES] = high.reshape(N, OWN, LANES)
            low = (acc - high.astype(F32)).astype(BF16)
            tgm[:, :, BOT + LANES :] = low.reshape(N, OWN, LANES)

    for d in FAR8:
        send(tgm.at[lax.rem(n + d, N)], tgr.at[d - 1], PH_TG, recv_sem.at[PH_TG], dev_n(d))
    wait_all(tgr, recv_sem.at[PH_TG])
    t = tgm[n].astype(F32)
    for d in range(N - 1):
        t = t + tgr[d].astype(F32)
    row_mass = jnp.sum(t[:, BOT : BOT + LANES] + t[:, BOT + LANES :], 1, keepdims=True)
    scale = 1.0 / (CROPS * row_mass)
    unit = unit_own[...]
    teacher = t[:, :BOT] + eg_less[...]
    ug = (eg_own[...] - teacher * (scale * CROPS)) * (1.0 / STUDENT_TEMP)
    radial = jnp.sum(unit * ug, 1, keepdims=True)
    bgall[n] = (inv_own[:, :1] * (ug - unit * radial)).astype(BF16)
    for d in FAR8:
        send(bgall.at[n], bgall.at[n], PH_BG, recv_sem.at[PH_BG], dev_n(d))
    wait_all(bgall.at[pl.ds(0, N - 1)], recv_sem.at[PH_BG])

    bg = bgall[...].reshape(ROWS, BOT)
    bts[...] = (
        lax.dot_general(perm[...], bg, NT, preferred_element_type=F32)
        .astype(BF16)
        .reshape(Y, GROUP, ROWS)
    )
    for d in FAR8:
        send(bts.at[lax.rem(y + d, Y)], btr.at[d - 1], PH_BT, bt_sem.at[d - 1], dev_y(d))
    gh_ref[...] = lax.dot_general(bg, wv[...], NT, preferred_element_type=F32).astype(BF16)
    wait_all(xall.at[pl.ds(0, Y - 1)], recv_sem.at[PH_X])
    gw = jnp.dot(bts[y], xall[y], preferred_element_type=F32)
    for d in NEAR8:
        wait_all(btr.at[d - 1], bt_sem.at[d - 1])
        gw = gw + jnp.dot(btr[d - 1], xall[lax.rem(y - d + Y, Y)], preferred_element_type=F32)
    gwf[...] = gw
    for i in range(Z):
        gwz[i, 0:4, :] = gwf[4 * i : 4 * i + 4, :LANES]
        gwz[i, 4:8, :] = gwf[4 * i : 4 * i + 4, LANES:]
    for d in FAR12:
        send(gwz.at[lax.rem(z + d, Z)], gwr.at[d - 1], PH_GW, recv_sem.at[PH_GW], dev_z(d))
    wait_all(brecv, send_sem.at[PH_B])
    wait_all(ball.at[pl.ds(0, N - 1)], send_sem.at[PH_U])
    wait_all(xall.at[pl.ds(0, Y - 1)], send_sem.at[PH_X])
    wait_all(egr, send_sem.at[PH_EG])
    wait_all(tgr, send_sem.at[PH_TG])
    wait_all(bgall.at[pl.ds(0, N - 1)], send_sem.at[PH_BG])
    wait_all(btr, send_sem.at[PH_BT])
    for it in range(ITERS):
        ph = PH_IT + 4 * it
        wait_all(yrecv.at[it], send_sem.at[ph])
        wait_all(zrecv.at[it], send_sem.at[ph + 1])
        wait_all(vall.at[it, pl.ds(0, Y - 1)], send_sem.at[ph + 2])
        if it < ITERS - 1:
            wait_all(nrecv.at[it], send_sem.at[ph + 3])
    wait_all(gwr, send_sem.at[PH_GW])
    wait_all(gwr, recv_sem.at[PH_GW])
    out = gwz[z]
    for d in range(Z - 1):
        out = out + gwr[d]
    gw_ref[:, :LANES] = out[:4]
    gw_ref[:, LANES:] = out[4:]


def shards(crop_hidden, bottleneck_weight, prototypes, teacher_scores):
    phases = 8 + 4 * ITERS
    vmem = pltpu.VMEM
    gh, gw = pl.pallas_call(
        kernel,
        out_shape=(
            pltpu.VMEM((ROWS, HIDB), BF16),
            pltpu.VMEM((4, HIDB), F32),
        ),
        in_specs=[pl.BlockSpec(memory_space=pltpu.HBM)] * 4,
        out_specs=(pl.BlockSpec(memory_space=vmem), pl.BlockSpec(memory_space=vmem)),
        scratch_shapes=[
            vmem((Y, ROWS, PIECE), BF16),
            vmem((Y, BOT, PIECE), BF16),
            vmem((HIDB, BOT), BF16),
            vmem((Y, ROWS, HIDB), BF16),
            vmem((Y * SUB, ROWS, LANES), F32),
            vmem((Y, SUB, LANES), F32),
            vmem((ITERS, Y, SUB, LANES), F32),
            vmem((ITERS, Y - 1, SUB, LANES), F32),
            vmem((ITERS, SUB, LANES), F32),
            vmem((ITERS, Z - 1, SUB, LANES), F32),
            vmem((ITERS, Y, SUB, LANES), F32),
            vmem((ITERS - 1, 8, LANES), F32),
            vmem((ITERS - 1, N - 1, 8, LANES), F32),
            vmem((ROWS, LANES), F32),
            vmem((ROWS, LANES), F32),
            vmem((N, OWN, BOT), F32),
            vmem((N - 1, OWN, BOT), F32),
            vmem((N, OWN, BOT), BF16),
            vmem((OWN, BOT), F32),
            vmem((OWN, LANES), F32),
            vmem((ROWS, PIECE), F32),
            vmem((ROWS, PIECE), BF16),
            vmem((N, OWN, WIDE), F32),
            vmem((N - 1, OWN, WIDE), F32),
            vmem((OWN, BOT), F32),
            vmem((OWN, BOT), F32),
            vmem((ROWS, BOT), F32),
            vmem((N, OWN, WIDE + LANES), BF16),
            vmem((N - 1, OWN, WIDE + LANES), BF16),
            vmem((N, OWN, BOT), BF16),
            vmem((BOT, BOT), BF16),
            vmem((Y, GROUP, ROWS), BF16),
            vmem((Y - 1, GROUP, ROWS), BF16),
            vmem((GROUP, HIDB), F32),
            vmem((Z, 8, LANES), F32),
            vmem((Z - 1, 8, LANES), F32),
            pltpu.SemaphoreType.DMA((2 + Y,)),
            pltpu.SemaphoreType.DMA((Y,)),
            pltpu.SemaphoreType.DMA((phases,)),
            pltpu.SemaphoreType.DMA((phases,)),
            pltpu.SemaphoreType.DMA((ITERS, Y - 1)),
            pltpu.SemaphoreType.DMA((Y - 1,)),
        ],
        compiler_params=pltpu.CompilerParams(
            collective_id=0, has_side_effects=True, vmem_limit_bytes=58 * 1024 * 1024
        ),
        name="sinkhorn_head",
    )(crop_hidden, bottleneck_weight, prototypes, teacher_scores)
    return gh, gw


def solution(mesh):
    placed = (P("wide", "narrow"), P("narrow", None), P(None, "narrow"), P("wide", "narrow"))
    return jax.shard_map(
        shards,
        mesh=mesh,
        in_specs=placed,
        out_specs=(P("wide", "narrow"), P("wide", "narrow")),
        check_vma=False,
    )
```

```python
import jax
import jax.numpy as jnp
from jax import lax
from jax.experimental import pallas as pl
from jax.experimental.pallas import tpu as pltpu
from jax.sharding import PartitionSpec as P

PROTO = 65536
CROPS = 12288
BOT = 384
ITERS = 3
TEACHER_TEMP = 0.07
STUDENT_TEMP = 0.1

Z, Y, N = 12, 8, 8
ROWS = CROPS // (Z * Y)
OWN = ROWS // N
COLS = PROTO // N
LANES = 128
PIECE = COLS // Y
SUB = PIECE // LANES
HALF = Y // 2
BSUB = 2 * SUB
HIDB = 2048 // N
WIDE = BOT + LANES
GROUPS = ROWS // 8
TOTALS = 1
GROUP = BOT // Y

F32 = jnp.float32
BF16 = jnp.bfloat16
MESH = pl.DeviceIdType.MESH

FAR8 = (4, 3, 5, 2, 6, 1, 7)
NEAR8 = (1, 7, 2, 6, 3, 5, 4)
BLOCKS = (0, 3, 1, 2)
NEXT = (1, 7, 2)
FAR12 = (6, 5, 7, 4, 8, 3, 9, 2, 10, 1, 11)
NT = (((1,), (1,)), ((), ()))


def kernel(
    x_hbm, w_hbm, p_hbm, t_hbm, gh_ref, gw_ref,
    tin, raw, wv, xall, texp, inv_col, cf, cbuf, yrecv, zsrc, zrecv, vall,
    nsrc, nrecv, ub, kappa, bpart, brecv, ball, unit_own, inv_own, sbuf, gbuf,
    egm, egr, eg_own, eg_less, tgf, tgm, tgr, bgall, perm, bts, btr, gwf, gwz, gwr,
    load_sem, proto_sem, send_sem, recv_sem, v_sem, bt_sem,
):
    w = lax.axis_index("wide")
    n = lax.axis_index("narrow")
    z = lax.div(w, Y)
    y = lax.rem(w, Y)

    def dev_y(d):
        return (z * Y + lax.rem(y + d, Y), n)

    def dev_z(d):
        return (lax.rem(z + d, Z) * Y + y, n)

    def dev_n(d):
        return (w, lax.rem(n + d, N))

    barrier = pltpu.get_barrier_semaphore()
    for d in FAR12:
        pl.semaphore_signal(barrier, inc=1, device_id=dev_z(d), device_id_type=MESH)
    for d in FAR8:
        pl.semaphore_signal(barrier, inc=1, device_id=dev_y(d), device_id_type=MESH)
    for d in FAR8:
        pl.semaphore_signal(barrier, inc=1, device_id=dev_n(d), device_id_type=MESH)

    blocks = [lax.rem(y + d, HALF) for d in BLOCKS]
    order = [2 * q + h for q in blocks for h in range(2)]
    load_x = pltpu.make_async_copy(x_hbm, xall.at[y], load_sem.at[0])
    load_w = pltpu.make_async_copy(w_hbm, wv, load_sem.at[1])

    def columns(p):
        return pl.ds(pl.multiple_of(p * PIECE, PIECE), PIECE)

    load_t = []
    for k, p in enumerate(order):
        load_t.append(
            pltpu.make_async_copy(t_hbm.at[:, columns(p)], tin.at[p], load_sem.at[2 + k])
        )
        load_t[-1].start()
    load_x.start()
    load_w.start()
    load_p = []
    for p in range(Y):
        load_p.append(
            pltpu.make_async_copy(p_hbm.at[:, columns(p)], raw.at[p], proto_sem.at[p])
        )
        load_p[-1].start()

    sends = []

    def send(src, dst, phase, sem, device):
        pltpu.make_async_remote_copy(
            src, dst, send_sem.at[phase], sem, device_id=device, device_id_type=MESH
        ).start()

    def wait_all(ref, sem):
        pltpu.make_async_copy(ref, ref, sem).wait()

    PH_B, PH_U, PH_X, PH_EG, PH_TG, PH_BG, PH_BT, PH_GW, PH_IT = range(9)

    def first_block(k):
        for h in range(2):
            p = order[2 * k + h]
            load_t[2 * k + h].wait()
            for s in range(SUB):
                e = jnp.exp(
                    tin[p, :, s * LANES : (s + 1) * LANES].astype(F32) * (1.0 / TEACHER_TEMP)
                )
                texp[p * SUB + s] = e
                row = h * SUB + s
                cf[k, row : row + 1, :] = jnp.sum(e, 0, keepdims=True)
        cbuf[0, blocks[k]] = cf[k].astype(BF16)

    def mass_block(it, k, rows):
        for s in range(BSUB):
            cf[k, s : s + 1, :] = jnp.sum(texp[blocks[k] * BSUB + s] * rows, 0, keepdims=True)
        cbuf[it, blocks[k]] = cf[k].astype(BF16)

    def send_columns(it, k):
        far = (BLOCKS[k] + HALF) % Y
        for d in (far, BLOCKS[k]) if far in (4, 5) else (BLOCKS[k], far):
            if d:
                send(
                    cbuf.at[it, blocks[k]], yrecv.at[it, d - 1],
                    PH_IT + 4 * it, recv_sem.at[PH_IT + 4 * it], dev_y(d),
                )

    def norm_piece(p):
        load_p[p].wait()
        for s in range(SUB):
            c = raw[p, :, s * LANES : (s + 1) * LANES].astype(F32)
            inv_col[p, s : s + 1, :] = lax.rsqrt(jnp.sum(c * c, 0, keepdims=True) + 1e-06)

    def own_rows():
        wait_all(brecv, recv_sem.at[PH_B])
        b = bpart[n]
        for d in range(N - 1):
            b = b + brecv[d]
        inv = lax.rsqrt(jnp.sum(b * b, 1, keepdims=True) + 1e-06)
        unit = b * inv
        unit_own[...] = unit
        inv_own[...] = jnp.broadcast_to(inv, (OWN, LANES))
        ball[n] = unit.astype(BF16)
        for d in FAR8:
            send(ball.at[n], ball.at[n], PH_U, recv_sem.at[PH_U], dev_n(d))

    def all_rows():
        wait_all(ball.at[pl.ds(0, N - 1)], recv_sem.at[PH_U])

    def student_piece(p):
        sbuf[...] = jnp.dot(
            ball[...].reshape(ROWS, BOT), raw[p], preferred_element_type=F32
        )
        total = jnp.zeros((ROWS, LANES), F32)
        for s in range(SUB):
            at = slice(s * LANES, (s + 1) * LANES)
            inv = inv_col[p, s : s + 1, :]
            e = jnp.exp(sbuf[:, at] * (inv * (1.0 / STUDENT_TEMP)))
            total = total + e
            gbuf[:, at] = (e * inv).astype(BF16)
        part = lax.dot_general(gbuf[...], raw[p], NT, preferred_element_type=F32)
        part = part.reshape(N, OWN, BOT)
        total = total.reshape(N, OWN, LANES)
        if p == 0:
            egm[:, :, :BOT] = part
            egm[:, :, BOT:] = total
        else:
            egm[:, :, :BOT] += part
            egm[:, :, BOT:] += total

    def send_student():
        for d in FAR8:
            send(egm.at[lax.rem(n + d, N)], egr.at[d - 1], PH_EG, recv_sem.at[PH_EG], dev_n(d))

    def own_student():
        wait_all(egr, recv_sem.at[PH_EG])
        e = egm[n]
        for d in range(N - 1):
            e = e + egr[d]
        total = jnp.sum(e[:, BOT:], 1, keepdims=True)
        eg_own[...] = e[:, :BOT] / total
        eg_less[...] = e[:, :BOT] * kappa[pl.ds(pl.multiple_of(n * OWN, OWN), OWN), :1]

    def permutation():
        k = lax.broadcasted_iota(jnp.int32, (BOT, BOT), 0)
        c = lax.broadcasted_iota(jnp.int32, (BOT, BOT), 1)
        per = GROUP // Z
        ky = lax.div(k, GROUP)
        kz = lax.div(lax.rem(k, GROUP), per)
        kb = lax.rem(k, per)
        perm[...] = jnp.where(c == kz * (per * Y) + ky * per + kb, 1.0, 0.0).astype(BF16)

    def row_tile(a, first):
        lane = lax.broadcasted_iota(jnp.int32, (8, LANES), 1)
        tile = jnp.zeros((8, LANES), F32)
        for g in range(GROUPS):
            mass = jnp.sum(a[8 * g : 8 * g + 8], 1, keepdims=True)
            tile = jnp.where(lane == first + g, mass, tile)
        return tile

    def share_hidden(*ds):
        for d in ds:
            send(xall.at[y], xall.at[y], PH_X, recv_sem.at[PH_X], dev_y(d))

    work = {
        (0, "y"): [lambda p=p: norm_piece(p) for p in range(Y)],
        (0, "z"): [lambda: share_hidden(1, 7, 2, 6), own_rows],
        (0, "v"): [all_rows, lambda: student_piece(0), lambda: student_piece(1)],
        (0, "n"): [lambda: student_piece(2), lambda: student_piece(3)],
        (1, "y"): [lambda: student_piece(4), lambda: student_piece(5)],
        (1, "z"): [
            lambda: share_hidden(3, 5),
            lambda: student_piece(6), lambda: student_piece(7), send_student,
        ],
        (1, "v"): [],
        (1, "n"): [permutation],
        (2, "y"): [own_student],
        (2, "z"): [lambda: share_hidden(4)],
        (2, "v"): [],
    }

    def beside(it, name):
        for item in work[(it, name)]:
            item()

    for it in range(ITERS):
        ph = PH_IT + 4 * it
        if it == 0:
            for k in range(2):
                first_block(k)
            pl.semaphore_wait(barrier, (Z - 1) + (Y - 1) + (N - 1))
            for k in range(2):
                send_columns(0, k)
            for k in range(2, HALF):
                first_block(k)
                send_columns(0, k)
            load_x.wait()
            load_w.wait()
            part = jnp.dot(xall[y], wv[...], preferred_element_type=F32)
            bpart[...] = part.reshape(N, OWN, BOT)
            for d in FAR8:
                send(bpart.at[lax.rem(n + d, N)], brecv.at[d - 1], PH_B, recv_sem.at[PH_B], dev_n(d))
        else:
            rows = ub[...]
            for k in range(HALF):
                mass_block(it, k, rows)
                send_columns(it, k)
        beside(it, "y")
        wait_all(yrecv.at[it], recv_sem.at[ph])
        mine = blocks[0]
        mass = cbuf[it, mine].astype(F32)
        for d in range(Y - 1):
            mass = mass + yrecv[it, d].astype(F32)
        zsrc[it] = mass.astype(BF16)
        for d in FAR12:
            send(zsrc.at[it], zrecv.at[it, d - 1], ph + 1, recv_sem.at[ph + 1], dev_z(d))
        beside(it, "z")
        wait_all(zrecv.at[it], recv_sem.at[ph + 1])
        for d in range(Z - 1):
            mass = mass + zrecv[it, d].astype(F32)
        vall[it, mine] = 1.0 / (PROTO * mass)
        for j in (2, 0, 1):
            send(vall.at[it, mine], vall.at[it, mine], ph + 2, v_sem.at[it, j], dev_y(NEXT[j]))
        beside(it, "v")

        acc = jnp.zeros((ROWS, LANES), F32)
        for k, d in enumerate((0,) + NEXT):
            q = lax.rem(y - d + Y, HALF)
            if k:
                wait_all(vall.at[it, q], v_sem.at[it, k - 1])
            if it < ITERS - 1:
                for s in range(BSUB):
                    acc = acc + texp[q * BSUB + s] * vall[it, q, s : s + 1, :]
                continue
            for h in range(2):
                p = 2 * q + h
                for s in range(SUB):
                    row = h * SUB + s
                    tv = texp[p * SUB + s] * vall[it, q, row : row + 1, :]
                    acc = acc + tv
                    gbuf[:, s * LANES : (s + 1) * LANES] = (tv * inv_col[p, s : s + 1, :]).astype(BF16)
                part = lax.dot_general(gbuf[...], raw[p], NT, preferred_element_type=F32)
                if k == 0 and h == 0:
                    tgf[...] = part
                else:
                    tgf[...] += part
        if it < ITERS - 1:
            tile = row_tile(acc, 0)
            if it == TOTALS:
                tile = tile + row_tile(egm[:, :, BOT:].reshape(ROWS, LANES), GROUPS)
            nsrc[it] = tile
            for d in FAR8:
                send(nsrc.at[it], nrecv.at[it, d - 1], ph + 3, recv_sem.at[ph + 3], dev_n(d))
            beside(it, "n")
            wait_all(nrecv.at[it], recv_sem.at[ph + 3])
            total = nsrc[it]
            for d in range(N - 1):
                total = total + nrecv[it, d]
            scale = 1.0 / (CROPS * total)
            for g in range(GROUPS):
                ub[8 * g : 8 * g + 8, :] = jnp.broadcast_to(scale[:, g : g + 1], (8, LANES))
            if it == TOTALS:
                for g in range(GROUPS):
                    ratio = scale[:, GROUPS + g : GROUPS + g + 1] / scale[:, g : g + 1]
                    kappa[8 * g : 8 * g + 8, :] = jnp.broadcast_to(ratio, (8, LANES))
        else:
            kap = kappa[...]
            for j in range(BOT // LANES):
                at = slice(j * LANES, (j + 1) * LANES)
                less = tgf[:, at] - kap * egm[:, :, at].reshape(ROWS, LANES)
                tgm[:, :, at] = less.astype(BF16).reshape(N, OWN, LANES)
            high = acc.astype(BF16)
            tgm[:, :, BOT : BOT + LANES] = high.reshape(N, OWN, LANES)
            low = (acc - high.astype(F32)).astype(BF16)
            tgm[:, :, BOT + LANES :] = low.reshape(N, OWN, LANES)

    for d in FAR8:
        send(tgm.at[lax.rem(n + d, N)], tgr.at[d - 1], PH_TG, recv_sem.at[PH_TG], dev_n(d))
    wait_all(tgr, recv_sem.at[PH_TG])
    t = tgm[n].astype(F32)
    for d in range(N - 1):
        t = t + tgr[d].astype(F32)
    row_mass = jnp.sum(t[:, BOT : BOT + LANES] + t[:, BOT + LANES :], 1, keepdims=True)
    scale = 1.0 / (CROPS * row_mass)
    unit = unit_own[...]
    teacher = t[:, :BOT] + eg_less[...]
    ug = (eg_own[...] - teacher * (scale * CROPS)) * (1.0 / STUDENT_TEMP)
    radial = jnp.sum(unit * ug, 1, keepdims=True)
    bgall[n] = (inv_own[:, :1] * (ug - unit * radial)).astype(BF16)
    for d in FAR8:
        send(bgall.at[n], bgall.at[n], PH_BG, recv_sem.at[PH_BG], dev_n(d))
    wait_all(bgall.at[pl.ds(0, N - 1)], recv_sem.at[PH_BG])

    bg = bgall[...].reshape(ROWS, BOT)
    bts[...] = (
        lax.dot_general(perm[...], bg, NT, preferred_element_type=F32)
        .astype(BF16)
        .reshape(Y, GROUP, ROWS)
    )
    for d in FAR8:
        send(bts.at[lax.rem(y + d, Y)], btr.at[d - 1], PH_BT, bt_sem.at[d - 1], dev_y(d))
    gh_ref[...] = lax.dot_general(bg, wv[...], NT, preferred_element_type=F32).astype(BF16)
    wait_all(xall.at[pl.ds(0, Y - 1)], recv_sem.at[PH_X])
    gw = jnp.dot(bts[y], xall[y], preferred_element_type=F32)
    for d in NEAR8:
        wait_all(btr.at[d - 1], bt_sem.at[d - 1])
        gw = gw + jnp.dot(btr[d - 1], xall[lax.rem(y - d + Y, Y)], preferred_element_type=F32)
    gwf[...] = gw
    for i in range(Z):
        gwz[i, 0:4, :] = gwf[4 * i : 4 * i + 4, :LANES]
        gwz[i, 4:8, :] = gwf[4 * i : 4 * i + 4, LANES:]
    for d in FAR12:
        send(gwz.at[lax.rem(z + d, Z)], gwr.at[d - 1], PH_GW, recv_sem.at[PH_GW], dev_z(d))
    wait_all(brecv, send_sem.at[PH_B])
    wait_all(ball.at[pl.ds(0, N - 1)], send_sem.at[PH_U])
    wait_all(xall.at[pl.ds(0, Y - 1)], send_sem.at[PH_X])
    wait_all(egr, send_sem.at[PH_EG])
    wait_all(tgr, send_sem.at[PH_TG])
    wait_all(bgall.at[pl.ds(0, N - 1)], send_sem.at[PH_BG])
    wait_all(btr, send_sem.at[PH_BT])
    for it in range(ITERS):
        ph = PH_IT + 4 * it
        wait_all(yrecv.at[it], send_sem.at[ph])
        wait_all(zrecv.at[it], send_sem.at[ph + 1])
        wait_all(vall.at[it, pl.ds(0, len(NEXT))], send_sem.at[ph + 2])
        if it < ITERS - 1:
            wait_all(nrecv.at[it], send_sem.at[ph + 3])
    wait_all(gwr, send_sem.at[PH_GW])
    wait_all(gwr, recv_sem.at[PH_GW])
    out = gwz[z]
    for d in range(Z - 1):
        out = out + gwr[d]
    gw_ref[:, :LANES] = out[:4]
    gw_ref[:, LANES:] = out[4:]


def shards(crop_hidden, bottleneck_weight, prototypes, teacher_scores):
    phases = 8 + 4 * ITERS
    vmem = pltpu.VMEM
    gh, gw = pl.pallas_call(
        kernel,
        out_shape=(
            pltpu.VMEM((ROWS, HIDB), BF16),
            pltpu.VMEM((4, HIDB), F32),
        ),
        in_specs=[pl.BlockSpec(memory_space=pltpu.HBM)] * 4,
        out_specs=(pl.BlockSpec(memory_space=vmem), pl.BlockSpec(memory_space=vmem)),
        scratch_shapes=[
            vmem((Y, ROWS, PIECE), BF16),
            vmem((Y, BOT, PIECE), BF16),
            vmem((HIDB, BOT), BF16),
            vmem((Y, ROWS, HIDB), BF16),
            vmem((Y * SUB, ROWS, LANES), F32),
            vmem((Y, SUB, LANES), F32),
            vmem((HALF, BSUB, LANES), F32),
            vmem((ITERS, HALF, BSUB, LANES), BF16),
            vmem((ITERS, Y - 1, BSUB, LANES), BF16),
            vmem((ITERS, BSUB, LANES), BF16),
            vmem((ITERS, Z - 1, BSUB, LANES), BF16),
            vmem((ITERS, HALF, BSUB, LANES), F32),
            vmem((ITERS - 1, 8, LANES), F32),
            vmem((ITERS - 1, N - 1, 8, LANES), F32),
            vmem((ROWS, LANES), F32),
            vmem((ROWS, LANES), F32),
            vmem((N, OWN, BOT), F32),
            vmem((N - 1, OWN, BOT), F32),
            vmem((N, OWN, BOT), BF16),
            vmem((OWN, BOT), F32),
            vmem((OWN, LANES), F32),
            vmem((ROWS, PIECE), F32),
            vmem((ROWS, PIECE), BF16),
            vmem((N, OWN, WIDE), F32),
            vmem((N - 1, OWN, WIDE), F32),
            vmem((OWN, BOT), F32),
            vmem((OWN, BOT), F32),
            vmem((ROWS, BOT), F32),
            vmem((N, OWN, WIDE + LANES), BF16),
            vmem((N - 1, OWN, WIDE + LANES), BF16),
            vmem((N, OWN, BOT), BF16),
            vmem((BOT, BOT), BF16),
            vmem((Y, GROUP, ROWS), BF16),
            vmem((Y - 1, GROUP, ROWS), BF16),
            vmem((GROUP, HIDB), F32),
            vmem((Z, 8, LANES), F32),
            vmem((Z - 1, 8, LANES), F32),
            pltpu.SemaphoreType.DMA((2 + Y,)),
            pltpu.SemaphoreType.DMA((Y,)),
            pltpu.SemaphoreType.DMA((phases,)),
            pltpu.SemaphoreType.DMA((phases,)),
            pltpu.SemaphoreType.DMA((ITERS, len(NEXT))),
            pltpu.SemaphoreType.DMA((Y - 1,)),
        ],
        compiler_params=pltpu.CompilerParams(
            collective_id=0, has_side_effects=True, vmem_limit_bytes=58 * 1024 * 1024
        ),
        name="sinkhorn_head",
    )(crop_hidden, bottleneck_weight, prototypes, teacher_scores)
    return gh, gw


def solution(mesh):
    placed = (P("wide", "narrow"), P("narrow", None), P(None, "narrow"), P("wide", "narrow"))
    return jax.shard_map(
        shards,
        mesh=mesh,
        in_specs=placed,
        out_specs=(P("wide", "narrow"), P("wide", "narrow")),
        check_vma=False,
    )
```

```python
import jax
import jax.numpy as jnp
from jax import lax
from jax.experimental import pallas as pl
from jax.experimental.pallas import tpu as pltpu
from jax.sharding import PartitionSpec as P

PROTO = 65536
CROPS = 12288
BOT = 384
ITERS = 3
TEACHER_TEMP = 0.07
STUDENT_TEMP = 0.1

Z, Y, N = 12, 8, 8
ROWS = CROPS // (Z * Y)
OWN = ROWS // N
COLS = PROTO // N
LANES = 128
PIECE = COLS // Y
SUB = PIECE // LANES
HALF = Y // 2
BSUB = 2 * SUB
HIDB = 2048 // N
WIDE = BOT + LANES
GROUPS = ROWS // 8
TOTALS = 1
GROUP = BOT // Y

F32 = jnp.float32
BF16 = jnp.bfloat16
MESH = pl.DeviceIdType.MESH

FAR8 = (4, 3, 5, 2, 6, 1, 7)
NEAR8 = (1, 7, 2, 6, 3, 5, 4)
BLOCKS = (0, 3, 1, 2)
NEXT = (1, 7, 2)
FAR12 = (6, 5, 7, 4, 8, 3, 9, 2, 10, 1, 11)
NT = (((1,), (1,)), ((), ()))


def kernel(
    x_hbm, w_hbm, p_hbm, t_hbm, gh_ref, gw_ref,
    tin, raw, wv, xall, texp, inv_col, cf, cbuf, yrecv, zsrc, zrecv, vall,
    nsrc, nrecv, ub, kappa, bpart, brecv, ball, unit_own, inv_own, sbuf, gbuf,
    egm, egr, eg_own, eg_less, tgf, tgm, tgr, bgall, perm, bts, btr, gwf, gwz, gwr,
    load_sem, proto_sem, send_sem, recv_sem, v_sem, bt_sem,
):
    w = lax.axis_index("wide")
    n = lax.axis_index("narrow")
    z = lax.div(w, Y)
    y = lax.rem(w, Y)

    def dev_y(d):
        return (z * Y + lax.rem(y + d, Y), n)

    def dev_z(d):
        return (lax.rem(z + d, Z) * Y + y, n)

    def dev_n(d):
        return (w, lax.rem(n + d, N))

    barrier = pltpu.get_barrier_semaphore()
    for d in FAR12:
        pl.semaphore_signal(barrier, inc=1, device_id=dev_z(d), device_id_type=MESH)
    for d in FAR8:
        pl.semaphore_signal(barrier, inc=1, device_id=dev_y(d), device_id_type=MESH)
    for d in FAR8:
        pl.semaphore_signal(barrier, inc=1, device_id=dev_n(d), device_id_type=MESH)

    blocks = [lax.rem(y + d, HALF) for d in BLOCKS]
    order = [2 * q + h for q in blocks for h in range(2)]
    load_x = pltpu.make_async_copy(x_hbm, xall.at[y], load_sem.at[0])
    load_w = pltpu.make_async_copy(w_hbm, wv, load_sem.at[1])

    def columns(p):
        return pl.ds(pl.multiple_of(p * PIECE, PIECE), PIECE)

    load_t = []
    for k, p in enumerate(order):
        load_t.append(
            pltpu.make_async_copy(t_hbm.at[:, columns(p)], tin.at[p], load_sem.at[2 + k])
        )
        load_t[-1].start()
    load_x.start()
    load_w.start()
    load_p = []
    for p in range(Y):
        load_p.append(
            pltpu.make_async_copy(p_hbm.at[:, columns(p)], raw.at[p], proto_sem.at[p])
        )
        load_p[-1].start()

    sends = []

    def send(src, dst, phase, sem, device):
        pltpu.make_async_remote_copy(
            src, dst, send_sem.at[phase], sem, device_id=device, device_id_type=MESH
        ).start()

    def wait_all(ref, sem):
        pltpu.make_async_copy(ref, ref, sem).wait()

    PH_B, PH_U, PH_X, PH_EG, PH_TG, PH_BG, PH_BT, PH_GW, PH_IT = range(9)

    def first_block(k):
        for h in range(2):
            p = order[2 * k + h]
            load_t[2 * k + h].wait()
            for s in range(SUB):
                e = jnp.exp(
                    tin[p, :, s * LANES : (s + 1) * LANES].astype(F32) * (1.0 / TEACHER_TEMP)
                )
                texp[p * SUB + s] = e
                row = h * SUB + s
                cf[k, row : row + 1, :] = jnp.sum(e, 0, keepdims=True)
        cbuf[0, blocks[k]] = cf[k].astype(BF16)

    def mass_block(it, k, rows):
        for s in range(BSUB):
            cf[k, s : s + 1, :] = jnp.sum(texp[blocks[k] * BSUB + s] * rows, 0, keepdims=True)
        cbuf[it, blocks[k]] = cf[k].astype(BF16)

    def send_columns(it, k):
        far = (BLOCKS[k] + HALF) % Y
        for d in (far, BLOCKS[k]) if far in (4, 5) else (BLOCKS[k], far):
            if d:
                send(
                    cbuf.at[it, blocks[k]], yrecv.at[it, d - 1],
                    PH_IT + 4 * it, recv_sem.at[PH_IT + 4 * it], dev_y(d),
                )

    def norm_piece(p):
        load_p[p].wait()
        for s in range(SUB):
            c = raw[p, :, s * LANES : (s + 1) * LANES].astype(F32)
            inv_col[p, s : s + 1, :] = lax.rsqrt(jnp.sum(c * c, 0, keepdims=True) + 1e-06)

    def own_rows():
        wait_all(brecv, recv_sem.at[PH_B])
        b = bpart[n]
        for d in range(N - 1):
            b = b + brecv[d]
        inv = lax.rsqrt(jnp.sum(b * b, 1, keepdims=True) + 1e-06)
        unit = b * inv
        unit_own[...] = unit
        inv_own[...] = jnp.broadcast_to(inv, (OWN, LANES))
        ball[n] = unit.astype(BF16)
        for d in FAR8:
            send(ball.at[n], ball.at[n], PH_U, recv_sem.at[PH_U], dev_n(d))

    def all_rows():
        wait_all(ball.at[pl.ds(0, N - 1)], recv_sem.at[PH_U])

    def student_piece(p):
        sbuf[...] = jnp.dot(
            ball[...].reshape(ROWS, BOT), raw[p], preferred_element_type=F32
        )
        total = jnp.zeros((ROWS, LANES), F32)
        for s in range(SUB):
            at = slice(s * LANES, (s + 1) * LANES)
            inv = inv_col[p, s : s + 1, :]
            e = jnp.exp(sbuf[:, at] * (inv * (1.0 / STUDENT_TEMP)))
            total = total + e
            gbuf[:, at] = (e * inv).astype(BF16)
        part = lax.dot_general(gbuf[...], raw[p], NT, preferred_element_type=F32)
        part = part.reshape(N, OWN, BOT)
        total = total.reshape(N, OWN, LANES)
        if p == 0:
            egm[:, :, :BOT] = part
            egm[:, :, BOT:] = total
        else:
            egm[:, :, :BOT] += part
            egm[:, :, BOT:] += total

    def send_student():
        for d in FAR8:
            send(egm.at[lax.rem(n + d, N)], egr.at[d - 1], PH_EG, recv_sem.at[PH_EG], dev_n(d))

    def own_student():
        wait_all(egr, recv_sem.at[PH_EG])
        e = egm[n]
        for d in range(N - 1):
            e = e + egr[d]
        total = jnp.sum(e[:, BOT:], 1, keepdims=True)
        eg_own[...] = e[:, :BOT] / total
        eg_less[...] = e[:, :BOT] * kappa[pl.ds(pl.multiple_of(n * OWN, OWN), OWN), :1]

    def permutation():
        k = lax.broadcasted_iota(jnp.int32, (BOT, BOT), 0)
        c = lax.broadcasted_iota(jnp.int32, (BOT, BOT), 1)
        per = GROUP // Z
        ky = lax.div(k, GROUP)
        kz = lax.div(lax.rem(k, GROUP), per)
        kb = lax.rem(k, per)
        perm[...] = jnp.where(c == kz * (per * Y) + ky * per + kb, 1.0, 0.0).astype(BF16)

    def row_tile(a, first):
        lane = lax.broadcasted_iota(jnp.int32, (8, LANES), 1)
        tile = jnp.zeros((8, LANES), F32)
        for g in range(GROUPS):
            mass = jnp.sum(a[8 * g : 8 * g + 8], 1, keepdims=True)
            tile = jnp.where(lane == first + g, mass, tile)
        return tile

    def share_hidden(*ds):
        for d in ds:
            send(xall.at[y], xall.at[y], PH_X, recv_sem.at[PH_X], dev_y(d))

    work = {
        (0, "y"): [lambda p=p: norm_piece(p) for p in range(Y)],
        (0, "z"): [lambda: share_hidden(1, 7, 2, 6), own_rows],
        (0, "v"): [all_rows, lambda: student_piece(0), lambda: student_piece(1)],
        (0, "n"): [lambda: student_piece(2), lambda: student_piece(3)],
        (1, "y"): [lambda: student_piece(4), lambda: student_piece(5)],
        (1, "z"): [
            lambda: share_hidden(3, 5),
            lambda: student_piece(6), lambda: student_piece(7), send_student,
        ],
        (1, "v"): [],
        (1, "n"): [permutation],
        (2, "y"): [own_student],
        (2, "z"): [lambda: share_hidden(4)],
        (2, "v"): [],
    }

    def beside(it, name):
        for item in work[(it, name)]:
            item()

    for it in range(ITERS):
        ph = PH_IT + 4 * it
        if it == 0:
            for k in range(2):
                first_block(k)
            pl.semaphore_wait(barrier, (Z - 1) + (Y - 1) + (N - 1))
            for k in range(2):
                send_columns(0, k)
            for k in range(2, HALF):
                first_block(k)
                send_columns(0, k)
            load_x.wait()
            load_w.wait()
            part = jnp.dot(xall[y], wv[...], preferred_element_type=F32)
            bpart[...] = part.reshape(N, OWN, BOT)
            for d in FAR8:
                send(bpart.at[lax.rem(n + d, N)], brecv.at[d - 1], PH_B, recv_sem.at[PH_B], dev_n(d))
        else:
            rows = ub[...]
            for k in range(HALF):
                mass_block(it, k, rows)
                send_columns(it, k)
        beside(it, "y")
        wait_all(yrecv.at[it], recv_sem.at[ph])
        mine = blocks[0]
        mass = cbuf[it, mine].astype(F32)
        for d in range(Y - 1):
            mass = mass + yrecv[it, d].astype(F32)
        zsrc[it] = mass.astype(BF16)
        for d in FAR12:
            send(zsrc.at[it], zrecv.at[it, d - 1], ph + 1, recv_sem.at[ph + 1], dev_z(d))
        beside(it, "z")
        wait_all(zrecv.at[it], recv_sem.at[ph + 1])
        for d in range(Z - 1):
            mass = mass + zrecv[it, d].astype(F32)
        vall[it, mine] = (1.0 / (PROTO * mass)).astype(BF16)
        for j in (2, 0, 1):
            send(vall.at[it, mine], vall.at[it, mine], ph + 2, v_sem.at[it, j], dev_y(NEXT[j]))
        beside(it, "v")

        acc = jnp.zeros((ROWS, LANES), F32)
        for k, d in enumerate((0,) + NEXT):
            q = lax.rem(y - d + Y, HALF)
            if k:
                wait_all(vall.at[it, q], v_sem.at[it, k - 1])
            v = vall[it, q].astype(F32)
            if it < ITERS - 1:
                for s in range(BSUB):
                    acc = acc + texp[q * BSUB + s] * v[s : s + 1]
                continue
            for h in range(2):
                p = 2 * q + h
                for s in range(SUB):
                    row = h * SUB + s
                    tv = texp[p * SUB + s] * v[row : row + 1]
                    acc = acc + tv
                    gbuf[:, s * LANES : (s + 1) * LANES] = (tv * inv_col[p, s : s + 1, :]).astype(BF16)
                part = lax.dot_general(gbuf[...], raw[p], NT, preferred_element_type=F32)
                if k == 0 and h == 0:
                    tgf[...] = part
                else:
                    tgf[...] += part
        if it < ITERS - 1:
            tile = row_tile(acc, 0)
            if it == TOTALS:
                tile = tile + row_tile(egm[:, :, BOT:].reshape(ROWS, LANES), GROUPS)
            nsrc[it] = tile
            for d in FAR8:
                send(nsrc.at[it], nrecv.at[it, d - 1], ph + 3, recv_sem.at[ph + 3], dev_n(d))
            beside(it, "n")
            wait_all(nrecv.at[it], recv_sem.at[ph + 3])
            total = nsrc[it]
            for d in range(N - 1):
                total = total + nrecv[it, d]
            scale = 1.0 / (CROPS * total)
            for g in range(GROUPS):
                ub[8 * g : 8 * g + 8, :] = jnp.broadcast_to(scale[:, g : g + 1], (8, LANES))
            if it == TOTALS:
                for g in range(GROUPS):
                    ratio = scale[:, GROUPS + g : GROUPS + g + 1] / scale[:, g : g + 1]
                    kappa[8 * g : 8 * g + 8, :] = jnp.broadcast_to(ratio, (8, LANES))
        else:
            kap = kappa[...]
            for j in range(BOT // LANES):
                at = slice(j * LANES, (j + 1) * LANES)
                less = tgf[:, at] - kap * egm[:, :, at].reshape(ROWS, LANES)
                tgm[:, :, at] = less.astype(BF16).reshape(N, OWN, LANES)
            high = acc.astype(BF16)
            tgm[:, :, BOT : BOT + LANES] = high.reshape(N, OWN, LANES)
            low = (acc - high.astype(F32)).astype(BF16)
            tgm[:, :, BOT + LANES :] = low.reshape(N, OWN, LANES)

    for d in FAR8:
        send(tgm.at[lax.rem(n + d, N)], tgr.at[d - 1], PH_TG, recv_sem.at[PH_TG], dev_n(d))
    wait_all(tgr, recv_sem.at[PH_TG])
    t = tgm[n].astype(F32)
    for d in range(N - 1):
        t = t + tgr[d].astype(F32)
    row_mass = jnp.sum(t[:, BOT : BOT + LANES] + t[:, BOT + LANES :], 1, keepdims=True)
    scale = 1.0 / (CROPS * row_mass)
    unit = unit_own[...]
    teacher = t[:, :BOT] + eg_less[...]
    ug = (eg_own[...] - teacher * (scale * CROPS)) * (1.0 / STUDENT_TEMP)
    radial = jnp.sum(unit * ug, 1, keepdims=True)
    bgall[n] = (inv_own[:, :1] * (ug - unit * radial)).astype(BF16)
    for d in FAR8:
        send(bgall.at[n], bgall.at[n], PH_BG, recv_sem.at[PH_BG], dev_n(d))
    wait_all(bgall.at[pl.ds(0, N - 1)], recv_sem.at[PH_BG])

    bg = bgall[...].reshape(ROWS, BOT)
    bts[...] = (
        lax.dot_general(perm[...], bg, NT, preferred_element_type=F32)
        .astype(BF16)
        .reshape(Y, GROUP, ROWS)
    )
    for d in FAR8:
        send(bts.at[lax.rem(y + d, Y)], btr.at[d - 1], PH_BT, bt_sem.at[d - 1], dev_y(d))
    gh_ref[...] = lax.dot_general(bg, wv[...], NT, preferred_element_type=F32).astype(BF16)
    wait_all(xall.at[pl.ds(0, Y - 1)], recv_sem.at[PH_X])
    gw = jnp.dot(bts[y], xall[y], preferred_element_type=F32)
    for d in NEAR8:
        wait_all(btr.at[d - 1], bt_sem.at[d - 1])
        gw = gw + jnp.dot(btr[d - 1], xall[lax.rem(y - d + Y, Y)], preferred_element_type=F32)
    gwf[...] = gw
    for i in range(Z):
        gwz[i, 0:4, :] = gwf[4 * i : 4 * i + 4, :LANES]
        gwz[i, 4:8, :] = gwf[4 * i : 4 * i + 4, LANES:]
    for d in FAR12:
        send(gwz.at[lax.rem(z + d, Z)], gwr.at[d - 1], PH_GW, recv_sem.at[PH_GW], dev_z(d))
    wait_all(brecv, send_sem.at[PH_B])
    wait_all(ball.at[pl.ds(0, N - 1)], send_sem.at[PH_U])
    wait_all(xall.at[pl.ds(0, Y - 1)], send_sem.at[PH_X])
    wait_all(egr, send_sem.at[PH_EG])
    wait_all(tgr, send_sem.at[PH_TG])
    wait_all(bgall.at[pl.ds(0, N - 1)], send_sem.at[PH_BG])
    wait_all(btr, send_sem.at[PH_BT])
    for it in range(ITERS):
        ph = PH_IT + 4 * it
        wait_all(yrecv.at[it], send_sem.at[ph])
        wait_all(zrecv.at[it], send_sem.at[ph + 1])
        wait_all(vall.at[it, pl.ds(0, len(NEXT))], send_sem.at[ph + 2])
        if it < ITERS - 1:
            wait_all(nrecv.at[it], send_sem.at[ph + 3])
    wait_all(gwr, send_sem.at[PH_GW])
    wait_all(gwr, recv_sem.at[PH_GW])
    out = gwz[z]
    for d in range(Z - 1):
        out = out + gwr[d]
    gw_ref[:, :LANES] = out[:4]
    gw_ref[:, LANES:] = out[4:]


def shards(crop_hidden, bottleneck_weight, prototypes, teacher_scores):
    phases = 8 + 4 * ITERS
    vmem = pltpu.VMEM
    gh, gw = pl.pallas_call(
        kernel,
        out_shape=(
            pltpu.VMEM((ROWS, HIDB), BF16),
            pltpu.VMEM((4, HIDB), F32),
        ),
        in_specs=[pl.BlockSpec(memory_space=pltpu.HBM)] * 4,
        out_specs=(pl.BlockSpec(memory_space=vmem), pl.BlockSpec(memory_space=vmem)),
        scratch_shapes=[
            vmem((Y, ROWS, PIECE), BF16),
            vmem((Y, BOT, PIECE), BF16),
            vmem((HIDB, BOT), BF16),
            vmem((Y, ROWS, HIDB), BF16),
            vmem((Y * SUB, ROWS, LANES), F32),
            vmem((Y, SUB, LANES), F32),
            vmem((HALF, BSUB, LANES), F32),
            vmem((ITERS, HALF, BSUB, LANES), BF16),
            vmem((ITERS, Y - 1, BSUB, LANES), BF16),
            vmem((ITERS, BSUB, LANES), BF16),
            vmem((ITERS, Z - 1, BSUB, LANES), BF16),
            vmem((ITERS, HALF, BSUB, LANES), BF16),
            vmem((ITERS - 1, 8, LANES), F32),
            vmem((ITERS - 1, N - 1, 8, LANES), F32),
            vmem((ROWS, LANES), F32),
            vmem((ROWS, LANES), F32),
            vmem((N, OWN, BOT), F32),
            vmem((N - 1, OWN, BOT), F32),
            vmem((N, OWN, BOT), BF16),
            vmem((OWN, BOT), F32),
            vmem((OWN, LANES), F32),
            vmem((ROWS, PIECE), F32),
            vmem((ROWS, PIECE), BF16),
            vmem((N, OWN, WIDE), F32),
            vmem((N - 1, OWN, WIDE), F32),
            vmem((OWN, BOT), F32),
            vmem((OWN, BOT), F32),
            vmem((ROWS, BOT), F32),
            vmem((N, OWN, WIDE + LANES), BF16),
            vmem((N - 1, OWN, WIDE + LANES), BF16),
            vmem((N, OWN, BOT), BF16),
            vmem((BOT, BOT), BF16),
            vmem((Y, GROUP, ROWS), BF16),
            vmem((Y - 1, GROUP, ROWS), BF16),
            vmem((GROUP, HIDB), F32),
            vmem((Z, 8, LANES), F32),
            vmem((Z - 1, 8, LANES), F32),
            pltpu.SemaphoreType.DMA((2 + Y,)),
            pltpu.SemaphoreType.DMA((Y,)),
            pltpu.SemaphoreType.DMA((phases,)),
            pltpu.SemaphoreType.DMA((phases,)),
            pltpu.SemaphoreType.DMA((ITERS, len(NEXT))),
            pltpu.SemaphoreType.DMA((Y - 1,)),
        ],
        compiler_params=pltpu.CompilerParams(
            collective_id=0, has_side_effects=True, vmem_limit_bytes=58 * 1024 * 1024
        ),
        name="sinkhorn_head",
    )(crop_hidden, bottleneck_weight, prototypes, teacher_scores)
    return gh, gw


def solution(mesh):
    placed = (P("wide", "narrow"), P("narrow", None), P(None, "narrow"), P("wide", "narrow"))
    return jax.shard_map(
        shards,
        mesh=mesh,
        in_specs=placed,
        out_specs=(P("wide", "narrow"), P("wide", "narrow")),
        check_vma=False,
    )
```
